256 devices in a mesh: dp: 2 (over x_hi), head: 2 (over x_lo), row: 64 (over y, z, core).
Axes of the slice: x: 4 (x_hi: 2, x_lo: 2; x = x_hi * 2 + x_lo), y: 4, z: 8, core: 2. Of those that a mesh axis runs over, the one named last changes fastest.
Arguments:
- pair_act: bfloat16 [1024, 512, 128], P(('dp', 'row')), parts along dimension 0, may hold values from -12 to 12
- chain_id: int32 [1024], P('dp'), parts along dimension 0, may hold values from 0 to 3, never falling along the last dimension, each value on 1 to 256 neighbouring positions
- residue_mask: int32 [1024], P('dp'), parts along dimension 0, may hold values 0 or 1
- norm_gain: float32 [128], replicated, may hold values from 0.5 to 1.5
- w_proj: bfloat16 [128, 4, 128], P(None, 'head'), may hold values from -1.25 to 1.25
- w_bias: bfloat16 [128, 4], P(None, 'head'), may hold values from -0.9 to 0.9
- chain_bias: float32 [2, 4], P(None, 'head'), may hold values from -2 to 2
- w_out: bfloat16 [4, 32, 128], P('head'), may hold values from -0.5 to 0.5
- w_dist: bfloat16 [128, 64], replicated, may hold values from -0.5 to 0.5
- dist_bias: float32 [64], replicated, may hold values from -3 to 3
Outputs:
- new_pair: bfloat16 [1024, 512, 128], P(('dp', 'row')), parts along dimension 0
- distogram: bfloat16 [1024, 512, 64], P(('dp', 'row')), parts along dimension 0
The draws below stay inside these ranges and needn't reach their ends.
There are 2 independent parts, one for each index of `dp`. The reference program is written for one: setup_inputs(seed, part) draws one part's arguments, and reference() takes and returns one part's arrays. A program takes and returns all parts, laid end to end along the dimension named above; an argument that names none is the same for every part. Nothing has to cross between parts.
Inputs may be any that keep to these rules, and one draw needn't show every extreme that they name: `chain_id`: chain ids never fall along the residues; no chain has more than half of the 512 residues.
All inputs are finite; a program needn't handle non-finite values.
Results may differ from the reference program's by a relative error of at most 0.013.
Values may be sent and summed in bfloat16 or wider, within the bound.
A program may use at most 64 MiB of HBM per device.

```python
import math
import jax
import jax.numpy as jnp
import numpy as np
from jax import lax

PAIR = 128
HEADS = 4
HEAD_DIM = 32
BINS = 64
N_RES = 512
N_HEAD = 2


def draw_pair_act(key, part):
    key = jax.random.fold_in(key, 5)
    first_key = jax.random.fold_in(key, 0)
    base = jax.random.normal(first_key, (N_RES, N_RES, PAIR), jnp.float32)
    return jnp.clip(base, -12.0, 12.0).astype(jnp.bfloat16)


def projection_block(key, spread):
    first_key, second_key = jax.random.split(key, 2)
    score_cols = jax.random.normal(first_key, (PAIR, HEADS, 2 * HEAD_DIM), jnp.float32) * (spread * PAIR ** (-0.5))
    other_cols = jax.random.normal(second_key, (PAIR, HEADS, 2 * HEAD_DIM), jnp.float32) * PAIR ** (-0.5)
    joined = jnp.concatenate([score_cols, other_cols], -1)
    return jnp.clip(joined, -1.25, 1.25).astype(jnp.bfloat16)


def draw_w_proj(key, part):
    key = jax.random.fold_in(key, 9)
    return projection_block(key, 2.83)


def draw_w_bias(key, part):
    key = jax.random.fold_in(key, 7)
    return jnp.clip(0.25 * jax.random.normal(key, (PAIR, HEADS), jnp.float32), -0.9, 0.9).astype(jnp.bfloat16)


def with_ends(array, stream_key, least, largest):
    longest = array.shape.index(max(array.shape))
    spots = []
    for shift in (0, 1):
        where = [jax.random.randint(jax.random.fold_in(stream_key, axis), (), 0, length) for axis, length in enumerate(array.shape)]
        where[longest] = (where[longest] + shift) % array.shape[longest]
        spots.append(tuple(where))
    return array.at[spots[0]].set(least).at[spots[1]].set(largest)


def block_scale(key, extent, cuts, least, top_value):
    loudness, own = 1.0, jax.random.fold_in(key, 6)
    for position, blocks in cuts:
        steps = jnp.exp(jax.random.uniform(jax.random.fold_in(own, position), (blocks,), jnp.float32, least / len(cuts), top_value / len(cuts)))
        loudness = loudness * jnp.repeat(steps, extent[position] // blocks).reshape([-1 if axis == position else 1 for axis in range(len(extent))])
    return loudness


def length_profile(count, total, reach, lean):
    loads = [(1 << 20) // math.isqrt(grade ** lean) + 1 for grade in range(2, count + 1)]
    rest, given = total - reach - (count - 1), [1] * (count - 1)
    while rest > 0:
        candidates = [i for i in range(count - 1) if given[i] < reach]
        whole, budget = sum([loads[i] for i in candidates]), rest
        for i in candidates:
            more = min(reach - given[i], max(1, budget * loads[i] // whole), rest)
            given[i] = given[i] + more
            rest = rest - more
    return np.array([reach] + given)


def ragged(rng, number_of, total, bound, skew):
    if number_of == 2:
        one = jax.random.randint(rng, (), max(1, total - bound), min(bound, total - 1) + 1)
        return jnp.stack([one, total - one])
    lengths = jnp.asarray(length_profile(number_of, total, bound, skew), jnp.int32)
    pairs = (number_of - 1) // 2
    donor, receiver = lengths[1:1 + 2 * pairs:2], lengths[2:2 + 2 * pairs:2]
    room = jnp.minimum(donor - 1, bound - receiver)
    shifted = jax.random.randint(jax.random.fold_in(rng, 1), (pairs,), 0, 1 << 20) % (room + 1)
    lengths = lengths.at[1:1 + 2 * pairs:2].set(donor - shifted).at[2:2 + 2 * pairs:2].set(receiver + shifted)
    return lengths[jax.random.permutation(jax.random.fold_in(rng, 2), number_of)]


def normal_values(stream_key, shape, deviation, reach, shards=(), held_as=jnp.bfloat16):
    gain = block_scale(stream_key, shape, shards, -0.22, 0.18) if shards else 1.0
    array = jax.random.normal(stream_key, shape, jnp.float32) * deviation * gain
    return jnp.minimum(jnp.maximum(array, -reach), reach).astype(held_as)


def setup_inputs(seed: int = 0, part: int = 0) -> dict:
    seeds = jax.random.split(jax.random.key(seed), 11)
    own_keys = jax.random.split(jax.random.fold_in(seeds[10], part), 11)
    pair_act = draw_pair_act(jax.random.fold_in(jax.random.fold_in(seeds[10], part), 71), part)
    chain_id = jnp.searchsorted(jnp.cumsum(ragged(own_keys[1], 4, N_RES, N_RES // 2, 1)), jnp.arange(N_RES), side="right").astype(jnp.int32)
    residue_mask = with_ends((jax.random.randint(own_keys[2], (N_RES,), 0, 8) < 7).astype(jnp.int32), jax.random.fold_in(own_keys[2], 1), 0, 1)
    norm_gain = jnp.clip(1.0 + 0.1 * jax.random.normal(seeds[3], (PAIR,), jnp.float32), 0.5, 1.5)
    w_proj = draw_w_proj(jax.random.fold_in(seeds[10], 71), part)
    w_bias = draw_w_bias(jax.random.fold_in(seeds[10], 71), part)
    chain_bias = jnp.clip(jax.random.uniform(seeds[6], (2, HEADS), jnp.float32, -2.0, 2.0) * block_scale(seeds[6], (2, HEADS), ((1, 2),), -0.4, 0.0), -2.0, 2.0)
    w_out = normal_values(seeds[7], (HEADS, HEAD_DIM, PAIR), (HEADS * HEAD_DIM) ** -0.5, 0.5, ((0, 2),))
    w_dist = normal_values(seeds[8], (PAIR, BINS), PAIR ** -0.5, 0.5)
    dist_bias = normal_values(seeds[9], (BINS,), 0.5, 3.0, (), jnp.float32)
    return {"pair_act": pair_act, "chain_id": chain_id, "residue_mask": residue_mask, "norm_gain": norm_gain, "w_proj": w_proj, "w_bias": w_bias, "chain_bias": chain_bias, "w_out": w_out, "w_dist": w_dist, "dist_bias": dist_bias}


def normalize(values, gain_vec):
    values = values.astype(jnp.float32)
    center_val = lax.optimization_barrier(jnp.mean(values, -1, keepdims=True))
    centered = values - center_val
    variance = lax.optimization_barrier(jnp.mean(centered * centered, -1, keepdims=True))
    return centered * lax.rsqrt(variance + 1e-05) * gain_vec

def reference(pair_act, chain_id, residue_mask, norm_gain, w_proj, w_bias, chain_bias, w_out, w_dist, dist_bias):
    pair_float = pair_act.astype(jnp.float32)
    normed = normalize(pair_float, norm_gain).astype(jnp.bfloat16)
    bias_kih = jnp.dot(normed, w_bias, preferred_element_type=jnp.float32).astype(jnp.bfloat16)
    bias_full = jnp.transpose(bias_kih, (2, 1, 0)).astype(jnp.float32)
    same_chain = chain_id[:, None] == chain_id[None, :]
    chain_term = jnp.where(same_chain[None], chain_bias[1][:, None, None], chain_bias[0][:, None, None])
    mask_term = (residue_mask.astype(jnp.float32) - 1.0) * 1000000000.0
    group_heads = HEADS // N_HEAD
    flat_w = w_proj.reshape(PAIR, HEADS * 4 * HEAD_DIM)
    out_groups = w_out.reshape(N_HEAD, group_heads, HEAD_DIM, PAIR).astype(jnp.float32)
    scaling = HEAD_DIM ** (-0.5)

    def column_step(column):
        projected = jnp.dot(column, flat_w, preferred_element_type=jnp.float32).astype(jnp.bfloat16)
        projected = projected.reshape(N_RES, HEADS, 4 * HEAD_DIM).astype(jnp.float32)
        queries = projected[..., :HEAD_DIM]
        keys_part = projected[..., HEAD_DIM:2 * HEAD_DIM]
        values_part = projected[..., 2 * HEAD_DIM:3 * HEAD_DIM]
        gate_part = projected[..., 3 * HEAD_DIM:]
        scores = jnp.einsum('ihd,khd->hik', queries, keys_part) * scaling
        scores = scores + bias_full + chain_term + mask_term[None, None, :]
        row_max = lax.optimization_barrier(jnp.max(scores, -1, keepdims=True))
        weights = jnp.exp(scores - row_max)
        softmax_w = (weights / lax.optimization_barrier(jnp.sum(weights, -1, keepdims=True))).astype(jnp.bfloat16)
        attended = jnp.einsum('hik,khd->ihd', softmax_w.astype(jnp.float32), values_part)
        gated = (jax.nn.sigmoid(gate_part) * attended).astype(jnp.bfloat16)
        grouped = gated.reshape(N_RES, N_HEAD, group_heads, HEAD_DIM).astype(jnp.float32)
        partials = jnp.einsum('ighd,ghdc->gic', grouped, out_groups).astype(jnp.bfloat16)
        partials = lax.optimization_barrier(partials)
        return lax.optimization_barrier(jnp.sum(partials.astype(jnp.float32), 0))
    columns_in = jnp.transpose(normed, (1, 0, 2))
    update = lax.map(column_step, columns_in)
    new_pair = (pair_float + jnp.transpose(update, (1, 0, 2))).astype(jnp.bfloat16)
    logits = (jnp.dot(new_pair, w_dist, preferred_element_type=jnp.float32) + dist_bias).astype(jnp.bfloat16)
    logits_float = logits.astype(jnp.float32)
    distogram = (logits_float + jnp.transpose(logits_float, (1, 0, 2))).astype(jnp.bfloat16)
    return (new_pair, distogram)
```

```python
import functools
import math

import jax
import jax.numpy as jnp
from jax import lax
from jax.experimental import pallas as pl
from jax.experimental.pallas import tpu as pltpu
from jax.sharding import PartitionSpec as P

MESH = pl.DeviceIdType.MESH
F32 = jnp.float32
BF16 = jnp.bfloat16
NT = (((1,), (1,)), ((), ()))
SCALE = 32.0**-0.5
SHAPE = {64: (4, 8), 8: (2, 2)}
PEERS_IN, BIAS_X, BIAS_Z, BIAS_Y, BIAS_C, W_P, W_O, OUT, FWD, LOG = 0, 2, 3, 4, 7, 8, 9, 10, 12, 14
N_SEM = 16


def layer_norm(values, gain):
    center = jnp.mean(values, -1, keepdims=True)
    centered = values - center
    variance = jnp.mean(centered * centered, -1, keepdims=True)
    return (centered * lax.rsqrt(variance + 1e-05) * gain).astype(BF16)


def kernel(
    ny,
    nz,
    x_ref,
    chain_ref,
    mask_ref,
    gain_ref,
    wproj_ref,
    wbias_ref,
    cbias_ref,
    wout_ref,
    wdist_ref,
    dbias_ref,
    new_ref,
    dist_ref,
    turn,
    xs,
    cols,
    gath,
    btab,
    bsc,
    wpg,
    wog,
    wre,
    wd2,
    qbuf,
    kbuf,
    vbuf,
    gbuf,
    pbuf,
    ns,
    rows,
    logc,
    ssem,
    rsem,
):
    nr = ny * nz * 2
    n = nr * 8
    ib = n // ny
    nb = nr // ny
    head = lax.axis_index("head")
    me = lax.axis_index("row")
    core = me % 2
    z = (me // 2) % nz
    y = me // (2 * nz)
    other = 1 - head

    def row_of(yy, zz, cc):
        return (yy * nz + zz) * 2 + cc

    def peer(idx):
        t = idx % nz
        rest = idx // nz
        sign = 2 * (t % 2) - 1
        dz = (sign * ((t + 1) // 2) + nz) % nz
        return row_of((y + rest // 2) % ny, (z + dz) % nz, (core + rest % 2) % 2)

    def to_row(src, dst, sem, target):
        return pltpu.make_async_remote_copy(
            src_ref=src,
            dst_ref=dst,
            send_sem=ssem.at[sem],
            recv_sem=rsem.at[sem],
            device_id={"row": target},
            device_id_type=MESH,
        )

    def to_other(src, dst, sem):
        return pltpu.make_async_remote_copy(
            src_ref=src,
            dst_ref=dst,
            send_sem=ssem.at[sem],
            recv_sem=rsem.at[sem],
            device_id={"head": other},
            device_id_type=MESH,
        )

    def wait_bytes(ref, sem):
        pltpu.make_async_copy(ref, ref, sem).wait()

    barrier = pltpu.get_barrier_semaphore()

    def greet(i, carry):
        pl.semaphore_signal(barrier, inc=1, device_id={"row": peer(i)}, device_id_type=MESH)
        return carry

    lax.fori_loop(1, nr, greet, 0)
    pl.semaphore_signal(barrier, inc=1, device_id={"head": other}, device_id_type=MESH)

    gain = gain_ref[...]

    def prepare(kk, carry):
        xk = x_ref[kk].astype(F32)
        turn[pl.ds(kk, n, stride=8), :] = xk
        nk = layer_norm(xk, gain)
        bk = lax.dot_general(wbias_ref[...], nk, NT, preferred_element_type=F32)
        bsc[0, pl.ds(kk, 1), :] = bk[0:1]
        bsc[1, pl.ds(kk, 1), :] = bk[1:2]
        return carry

    lax.fori_loop(0, 8, prepare, 0)
    def pick(i, carry):
        for hf in range(2):
            for j in range(nb // 2):
                r = i * (nb // 2) + j
                part = turn[pl.ds(pl.multiple_of(r * 64 + (4 * head + 2 * hf) * 8, 16), 16), :]
                xs[hf, r] = part.astype(BF16)
        return carry

    lax.fori_loop(0, 2 * ny, pick, 0)

    ids = chain_ref[...]
    lane = lax.broadcasted_iota(jnp.int32, (8, n), 1)
    sub = lax.broadcasted_iota(jnp.int32, (8, n), 0)
    mine = lane == sub + me * 8
    my_ids = jnp.sum(jnp.where(mine, ids, 0), -1, keepdims=True)
    my_mask = jnp.sum(jnp.where(mine, mask_ref[...], 0), -1, keepdims=True)
    mask_term = (my_mask.astype(F32) - 1.0) * 1000000000.0
    same = my_ids == ids
    blocks = []
    for hh in range(2):
        chain_term = jnp.where(same, cbias_ref[1, hh], cbias_ref[0, hh])
        blocks.append((bsc[hh] + chain_term + mask_term) * (1.0 / SCALE))
    gath[core, y, z, head] = jnp.concatenate(blocks, 0).astype(BF16)

    pl.semaphore_wait(barrier, nr)

    def send_cols(hf):
        def send(i, carry):
            q = peer(i)
            to_row(xs.at[hf, q], cols.at[hf, me], PEERS_IN + hf, q).start()
            return carry

        lax.fori_loop(1, nr, send, 0)
        pltpu.make_async_copy(xs.at[hf, me], cols.at[hf, me], rsem.at[PEERS_IN + hf]).start()

    own_block = gath.at[core, y, z, head]
    bias_x = to_other(own_block, own_block, BIAS_X)
    bias_x.start()
    w_p = to_other(wproj_ref, wpg, W_P)
    w_p.start()
    w_o = to_other(wout_ref, wog, W_O)
    w_o.start()
    send_cols(0)
    bias_x.wait()
    for d in range(1, nz):
        to_row(gath.at[core, y, z], gath.at[core, y, z], BIAS_Z, row_of(y, (z + d) % nz, core)).start()
    send_cols(1)
    sib = row_of(y, z, 1 - core)
    wait_bytes(gath.at[0, 0, pl.ds(0, nz - 1)], rsem.at[BIAS_Z])
    wait_bytes(gath.at[0, 0, pl.ds(0, nz - 1)], ssem.at[BIAS_Z])
    for d in range(1, ny):
        to_row(gath.at[core, y], gath.at[core, y], BIAS_Y + d - 1, row_of((y + d) % ny, z, core)).start()
    to_row(gath.at[core, y], gath.at[core, y], BIAS_C, sib).start()
    for d in range(1, ny):
        from_y = (y + ny - d) % ny
        wait_bytes(gath.at[core, from_y], rsem.at[BIAS_Y + d - 1])
        to_row(gath.at[core, from_y], gath.at[core, from_y], BIAS_C, sib).start()

    w_p.wait()
    w_o.wait()
    li = lax.broadcasted_iota(jnp.int32, (128, 128), 0)
    mi = lax.broadcasted_iota(jnp.int32, (128, 128), 1)
    for t in range(4):
        total = jnp.zeros((128, 128), F32)
        for hh in range(2):
            for which, ref in ((head, wproj_ref), (other, wpg)):
                h = 2 * which + hh
                pick = (mi // 32 == h) & (li == t * 32 + mi % 32)
                total += jnp.dot(
                    ref[:, hh * 128 : (hh + 1) * 128], pick.astype(BF16), preferred_element_type=F32
                )
        wre[t] = total.astype(BF16)
    wre[4, pl.ds(pl.multiple_of(head * 64, 64), 64), :] = wout_ref[...]
    wre[4, pl.ds(pl.multiple_of(other * 64, 64), 64), :] = wog[...]
    wd = wdist_ref[...].astype(F32)
    zero = jnp.zeros_like(wd)
    wd2[...] = jnp.concatenate(
        [jnp.concatenate([wd, zero], 1), jnp.concatenate([zero, wd], 1)], 0
    ).astype(BF16)
    db = dbias_ref[...]
    db2 = jnp.concatenate([db, db], 1)
    wide = lax.broadcasted_iota(jnp.int32, (n, 128), 1)
    for h in range(4):
        ones = jnp.where(wide // 32 == h, 1.0, 0.0).astype(BF16)
        for c in range(2):
            vbuf[c, h * n : (h + 1) * n, 128:] = ones

    def project(hf):
        def chunk(q, carry):
            at = pl.multiple_of(q * nb, nb)
            out = pl.ds(pl.multiple_of(q * ib, ib), ib)
            values = cols[hf, pl.ds(at, nb)].astype(F32).reshape(nb * 16, 128)
            normed = layer_norm(values, gain)
            for t in range(4):
                pt = jnp.dot(normed, wre[t], preferred_element_type=F32)
                pt = pt.reshape(nb, 2, 8, 128)
                for c in range(2):
                    val = pt[:, c].reshape(ib, 128)
                    if t == 0:
                        qbuf[c, out, :] = val.astype(BF16)
                    elif t == 1:
                        kbuf[c, out, :] = val.astype(BF16)
                    elif t == 2:
                        lanes = lax.broadcasted_iota(jnp.int32, (ib, 128), 1) // 32
                        for h in range(4):
                            vbuf[c, pl.ds(pl.multiple_of(h * n + q * ib, ib), ib), :128] = jnp.where(
                                lanes == h, val, 0.0
                            ).astype(BF16)
                    else:
                        gbuf[c, out, :] = jax.nn.sigmoid(val.astype(BF16).astype(F32))
            return carry

        lax.fori_loop(0, ny, chunk, 0)

    def repack(q, carry):
        at = pl.ds(pl.multiple_of(q * ib, ib), ib)
        for a in range(2):
            g0 = gath[0, q, :, a].astype(F32)
            g1 = gath[1, q, :, a].astype(F32)
            for hh in range(2):
                both = jnp.concatenate(
                    [g0[:, hh * 8 : hh * 8 + 8], g1[:, hh * 8 : hh * 8 + 8]], 1
                ).astype(BF16).reshape(ib, n)
                for b in range(ny):
                    btab[b, 2 * a + hh, at, :] = both[:, b * ib : (b + 1) * ib]
        return carry

    eye = (
        lax.broadcasted_iota(jnp.int32, (ib, ib), 0) == lax.broadcasted_iota(jnp.int32, (ib, ib), 1)
    ).astype(F32).astype(BF16)
    qlane = lax.broadcasted_iota(jnp.int32, (ib, 128), 1) // 32

    def attend(hf, b):
        at = pl.ds(pl.multiple_of(b * ib, ib), ib)
        blk = pl.ds(pl.multiple_of(b * nb, nb), nb)
        before = cols[hf, blk].astype(F32)
        after = []
        for c in range(2):
            q = qbuf[c, at, :]
            for h in range(4):
                qm = jnp.where(qlane == h, q, jnp.zeros_like(q))
                lhs = jnp.concatenate([qm, eye], 1)
                rhs = jnp.concatenate([kbuf[c], btab[b, h]], 1)
                s = lax.dot_general(lhs, rhs, NT, preferred_element_type=F32)
                top = jnp.max(s, -1, keepdims=True)
                pbuf[c, :, h * n : (h + 1) * n] = jnp.exp2(
                    (s - top) * (SCALE * math.log2(math.e))
                ).astype(BF16)
            nd = jnp.dot(pbuf[c], vbuf[c], preferred_element_type=F32)
            gated = (gbuf[c, at, :] * (nd[:, :128] / nd[:, 128:])).astype(BF16)
            upd = jnp.dot(gated, wre[4], preferred_element_type=F32)
            after.append(before[:, c * 8 : c * 8 + 8] + upd.reshape(nb, 8, 128))
        ns[hf, blk] = jnp.concatenate(after, 1).astype(BF16)
        flat = jnp.concatenate([v.reshape(ib, 128).astype(BF16) for v in after], 1)
        logits = jnp.dot(flat, wd2[...], preferred_element_type=F32) + db2
        logc[head, hf, at, :] = logits.astype(BF16)

    def forward(hf):
        wait_bytes(rows.at[head, hf], rsem.at[OUT + hf])
        to_other(rows.at[head, hf], rows.at[head, hf], FWD + hf).start()

    def half(hf, carry):
        wait_bytes(cols.at[hf], rsem.at[PEERS_IN + hf])
        project(hf)

        @pl.when(hf == 0)
        def _():
            wait_bytes(gath.at[0], rsem.at[BIAS_C])
            lax.fori_loop(0, ny, repack, 0)

        def step(t, c2):
            b = (y + t) % ny
            attend(hf, b)

            def send(j, c3):
                target = b * nb + (me % nb + j) % nb
                to_row(ns.at[hf, target], rows.at[head, hf, me], OUT + hf, target).start()
                return c3

            lax.fori_loop(jnp.where(t == 0, 1, 0), nb, send, 0)

            @pl.when(t == 0)
            def _():
                pltpu.make_async_copy(
                    ns.at[hf, me], rows.at[head, hf, me], rsem.at[OUT + hf]
                ).start()

            @pl.when((hf == 1) & (t == ny // 2))
            def _():
                forward(0)

            return c2

        lax.fori_loop(0, ny, step, 0)
        to_other(logc.at[head, hf], logc.at[head, hf], LOG + hf).start()
        return carry

    lax.fori_loop(0, 2, half, 0)
    forward(1)

    def place(a, hf):
        def block(i, carry):
            for j in range(nb // 2):
                r = i * (nb // 2) + j
                at = pl.ds(pl.multiple_of(r * 64 + (4 * a + 2 * hf) * 8, 16), 16)
                turn[at, :] = rows[a, hf, r].astype(F32)
            return carry

        lax.fori_loop(0, 2 * ny, block, 0)

    for hf in range(2):
        place(head, hf)
    for hf in range(2):
        wait_bytes(rows.at[other, hf], rsem.at[FWD + hf])
        place(other, hf)
        wait_bytes(logc.at[other, hf], rsem.at[LOG + hf])
    for kk in range(8):
        new = turn[pl.ds(kk, n, stride=8), :].astype(BF16)
        new_ref[kk] = new
        own = (jnp.dot(new, wdist_ref[...], preferred_element_type=F32) + db).astype(BF16)
        c = kk % 2
        mirrored = logc[kk // 4, (kk // 2) % 2][:, c * 64 : (c + 1) * 64]
        dist_ref[kk] = (own.astype(F32) + mirrored.astype(F32)).astype(BF16)

    for hf in range(2):
        wait_bytes(xs.at[hf, pl.ds(0, nr - 1)], ssem.at[PEERS_IN + hf])
        wait_bytes(xs.at[hf, pl.ds(0, nr - 1)], ssem.at[OUT + hf])
        wait_bytes(rows.at[head, hf], ssem.at[FWD + hf])
        wait_bytes(logc.at[head, hf], ssem.at[LOG + hf])
    for d in range(1, ny):
        wait_bytes(gath.at[core, y], ssem.at[BIAS_Y + d - 1])
    wait_bytes(gath.at[core], ssem.at[BIAS_C])


def shards(
    pair_act,
    chain_id,
    residue_mask,
    norm_gain,
    w_proj,
    w_bias,
    chain_bias,
    w_out,
    w_dist,
    dist_bias,
):
    _, n, width = pair_act.shape
    nr = n // 8
    ny, nz = SHAPE[nr]
    bins = w_dist.shape[1]
    ib = n // ny
    wb = jnp.zeros((16, width), BF16).at[:2].set(w_bias.T)
    vmem = pl.BlockSpec(memory_space=pltpu.VMEM)
    smem = pl.BlockSpec(memory_space=pltpu.SMEM)
    return pl.pallas_call(
        functools.partial(kernel, ny, nz),
        out_shape=(
            jax.ShapeDtypeStruct((8, n, width), BF16),
            jax.ShapeDtypeStruct((8, n, bins), BF16),
        ),
        in_specs=[vmem, vmem, vmem, vmem, vmem, vmem, smem, vmem, vmem, vmem],
        out_specs=(vmem, vmem),
        scratch_shapes=[
            pltpu.VMEM((n * 8, width), F32),
            pltpu.VMEM((2, nr, 16, width), BF16),
            pltpu.VMEM((2, nr, 16, width), BF16),
            pltpu.VMEM((2, ny, nz, 2, 16, n), BF16),
            pltpu.VMEM((ny, 4, n, ib), BF16),
            pltpu.VMEM((2, 8, n), F32),
            pltpu.VMEM((width, 256), BF16),
            pltpu.VMEM((64, width), BF16),
            pltpu.VMEM((5, width, width), BF16),
            pltpu.VMEM((2 * width, 2 * bins), BF16),
            pltpu.VMEM((2, n, width), BF16),
            pltpu.VMEM((2, n, width), BF16),
            pltpu.VMEM((2, 4 * n, 2 * width), BF16),
            pltpu.VMEM((2, n, width), F32),
            pltpu.VMEM((2, ib, 4 * n), BF16),
            pltpu.VMEM((2, nr, 16, width), BF16),
            pltpu.VMEM((2, 2, nr, 16, width), BF16),
            pltpu.VMEM((2, 2, n, 2 * bins), BF16),
            pltpu.SemaphoreType.DMA((N_SEM,)),
            pltpu.SemaphoreType.DMA((N_SEM,)),
        ],
        compiler_params=pltpu.CompilerParams(
            collective_id=0, has_side_effects=True, vmem_limit_bytes=48 << 20
        ),
        name="triangle",
    )(
        pair_act,
        chain_id.reshape(1, n),
        residue_mask.reshape(1, n),
        norm_gain.reshape(1, width),
        w_proj.reshape(width, 256),
        wb,
        chain_bias,
        w_out.reshape(64, width),
        w_dist,
        dist_bias.reshape(1, bins),
    )


def solution(mesh):
    in_specs = (
        P(("dp", "row"), None, None),
        P("dp"),
        P("dp"),
        P(),
        P(None, "head", None),
        P(None, "head"),
        P(None, "head"),
        P("head", None, None),
        P(),
        P(),
    )
    out_specs = (P(("dp", "row"), None, None), P(("dp", "row"), None, None))
    return jax.shard_map(shards, mesh=mesh, in_specs=in_specs, out_specs=out_specs, check_vma=False)
```

```python
import functools
import math

import jax
import jax.numpy as jnp
from jax import lax
from jax.experimental import pallas as pl
from jax.experimental.pallas import tpu as pltpu
from jax.sharding import PartitionSpec as P

MESH = pl.DeviceIdType.MESH
F32 = jnp.float32
BF16 = jnp.bfloat16
NT = (((1,), (1,)), ((), ()))
TN = (((0,), (0,)), ((), ()))
SCALE = 32.0**-0.5
SHAPE = {64: (4, 8), 8: (2, 2)}
PEERS_IN, BIAS_Z, BIAS_Y, BIAS_X, BIAS_C, W_P, W_O, LOG, X_IN, OUT, FWD = 0, 4, 5, 17, 21, 25, 26, 27, 28, 29, 33
N_SEM = 37


def layer_norm(values, gain):
    center = jnp.mean(values, -1, keepdims=True)
    centered = values - center
    variance = jnp.mean(centered * centered, -1, keepdims=True)
    return (centered * lax.rsqrt(variance + 1e-05) * gain).astype(BF16)


def kernel(
    ny,
    nz,
    x_ref,
    chain_ref,
    mask_ref,
    gain_ref,
    wproj_ref,
    wbias_ref,
    cbias_ref,
    wout_ref,
    wdist_ref,
    dbias_ref,
    rows,
    logc,
    xbuf,
    turn,
    xs,
    cols,
    gath,
    btab,
    bsc,
    wpg,
    wog,
    wre,
    qbuf,
    kbuf,
    vbuf,
    gbuf,
    ns,
    own_log,
    ssem,
    rsem,
):
    nr = ny * nz * 2
    n = nr * 8
    ib = n // ny
    nb = nr // ny
    bins = wdist_ref.shape[0]
    head = lax.axis_index("head")
    me = lax.axis_index("row")
    core = me % 2
    z = (me // 2) % nz
    y = me // (2 * nz)
    other = 1 - head

    def row_of(yy, zz, cc):
        return (yy * nz + zz) * 2 + cc

    def peer(idx):
        t = idx % nz
        rest = idx // nz
        sign = 2 * (t % 2) - 1
        dz = (sign * ((t + 1) // 2) + nz) % nz
        return row_of((y + rest // 2) % ny, (z + dz) % nz, (core + rest % 2) % 2)

    def to_row(src, dst, sem, target):
        return pltpu.make_async_remote_copy(
            src_ref=src,
            dst_ref=dst,
            send_sem=ssem.at[sem],
            recv_sem=rsem.at[sem],
            device_id={"row": target},
            device_id_type=MESH,
        )

    def to_other(src, dst, sem):
        return pltpu.make_async_remote_copy(
            src_ref=src,
            dst_ref=dst,
            send_sem=ssem.at[sem],
            recv_sem=rsem.at[sem],
            device_id={"head": other},
            device_id_type=MESH,
        )

    def wait_bytes(ref, sem):
        pltpu.make_async_copy(ref, ref, sem).wait()

    pltpu.make_async_copy(x_ref, xbuf, rsem.at[X_IN]).start()

    barrier = pltpu.get_barrier_semaphore()

    def greet(i, carry):
        pl.semaphore_signal(barrier, inc=1, device_id={"row": peer(i)}, device_id_type=MESH)
        return carry

    lax.fori_loop(1, nr, greet, 0)
    pl.semaphore_signal(barrier, inc=1, device_id={"head": other}, device_id_type=MESH)

    gain = gain_ref[...]

    pltpu.make_async_copy(x_ref, xbuf, rsem.at[X_IN]).wait()

    def prepare(kk, carry):
        xk = xbuf[kk].astype(F32)
        turn[pl.ds(kk, n, stride=8), :] = xk
        nk = layer_norm(xk, gain)
        bk = lax.dot_general(wbias_ref[...], nk, NT, preferred_element_type=F32)
        bsc[0, pl.ds(kk, 1), :] = bk[0:1]
        bsc[1, pl.ds(kk, 1), :] = bk[1:2]
        return carry

    lax.fori_loop(0, 8, prepare, 0)
    def pick(i, carry):
        for j in range(nb // 2):
            r = i * (nb // 2) + j
            xs[r] = turn[pl.ds(pl.multiple_of(r * 64 + head * 32, 32), 32), :].astype(BF16)
        return carry

    lax.fori_loop(0, 2 * ny, pick, 0)

    ids = chain_ref[...]
    lane = lax.broadcasted_iota(jnp.int32, (8, n), 1)
    sub = lax.broadcasted_iota(jnp.int32, (8, n), 0)
    mine = lane == sub + me * 8
    my_ids = jnp.sum(jnp.where(mine, ids, 0), -1, keepdims=True)
    my_mask = jnp.sum(jnp.where(mine, mask_ref[...], 0), -1, keepdims=True)
    mask_term = (my_mask.astype(F32) - 1.0) * 1000000000.0
    same = my_ids == ids
    blocks = []
    for hh in range(2):
        chain_term = jnp.where(same, cbias_ref[1, hh], cbias_ref[0, hh])
        blocks.append((bsc[hh] + chain_term + mask_term) * (1.0 / SCALE))
    block = jnp.concatenate(blocks, 0).astype(BF16)
    for b in range(ny):
        gath[core, head, y, b, z] = block[:, b * ib : (b + 1) * ib]

    pl.semaphore_wait(barrier, nr)

    def send_cols(i, carry):
        q = peer(i)
        to_row(xs.at[q], cols.at[me], PEERS_IN + i // nb, q).start()
        return carry

    def bias_z():
        part = gath.at[core, head, y, :, z]
        for d in range(1, nz):
            to_row(part, part, BIAS_Z, row_of(y, (z + d) % nz, core)).start()

    def bias_y(t):
        for d in range(1, ny):
            part = gath.at[core, head, y, (y + d + t + 1) % ny]
            to_row(part, part, BIAS_Y + t * (ny - 1) + d - 1, row_of((y + d) % ny, z, core)).start()

    sib = row_of(y, z, 1 - core)

    def after_y(t):
        b = (y + t + 1) % ny
        for d in range(1, ny):
            wait_bytes(
                gath.at[core, head, (y + ny - d) % ny, b], rsem.at[BIAS_Y + t * (ny - 1) + d - 1]
            )
        part = gath.at[core, head, :, b]
        to_other(part, part, BIAS_X + t).start()
        to_row(part, part, BIAS_C + t, sib).start()

    def after_x(t):
        part = gath.at[core, other, :, (y + t + 1) % ny]
        wait_bytes(part, rsem.at[BIAS_X + t])
        to_row(part, part, BIAS_C + t, sib).start()

    bias_z()
    w_p = to_other(wproj_ref, wpg, W_P)
    w_p.start()
    w_o = to_other(wout_ref, wog, W_O)
    w_o.start()
    lax.fori_loop(1, nr, send_cols, 0)
    pltpu.make_async_copy(xs.at[me], cols.at[me], rsem.at[PEERS_IN]).start()

    li = lax.broadcasted_iota(jnp.int32, (128, 128), 0)
    mi = lax.broadcasted_iota(jnp.int32, (128, 128), 1)
    shift = li - mi
    mh = mi // 32
    ri = lax.broadcasted_iota(jnp.int32, (128, 256), 0) * 2
    rj = lax.broadcasted_iota(jnp.int32, (128, 256), 1)

    def arrange(which, ref):
        total = [jnp.zeros((128, 128), F32) for _ in range(4)]
        for hh in range(2):
            h = 2 * which + hh
            split = jnp.where(rj == ri + hh, 1.0, 0.0).astype(BF16)
            w = jnp.dot(split, ref[...], preferred_element_type=F32).astype(BF16)
            for t in range(4):
                pick = jnp.where((shift == 32 * (t - h)) & (mh == h), 1.0, 0.0).astype(BF16)
                total[t] += jnp.dot(w, pick, preferred_element_type=F32)
        return total

    mine_w = arrange(head, wproj_ref)
    for t in range(4):
        wre[t] = mine_w[t].astype(BF16)
    wre[4, pl.ds(pl.multiple_of(head * 64, 64), 64), :] = wout_ref[...]
    bi = lax.broadcasted_iota(jnp.int32, (bins, bins), 0)
    bj = lax.broadcasted_iota(jnp.int32, (bins, bins), 1)
    db = jnp.sum(jnp.where(bi == bj, dbias_ref[...], 0.0), -1, keepdims=True)
    for c in range(4):
        for pair in range(2):
            vbuf[c, pair, 64:, :] = jnp.ones((16, n), BF16)

    wait_bytes(gath.at[0, 0, 0, :, pl.ds(0, nz - 1)], rsem.at[BIAS_Z])
    for t in range(ny):
        bias_y(t)
    w_p.wait()
    w_o.wait()
    their_w = arrange(other, wpg)
    for t in range(4):
        full = wre[t].astype(F32) + their_w[t]
        wre[t] = (full if t == 1 else jnp.transpose(full)).astype(BF16)
    wre[4, pl.ds(pl.multiple_of(other * 64, 64), 64), :] = wog[...]
    after_y(0)
    after_y(1)
    after_x(0)

    def project():
        def chunk(d, carry):
            q = (y + ny - d) % ny
            wait_bytes(cols.at[pl.ds(q * nb, nb)], rsem.at[PEERS_IN + d])
            at = pl.multiple_of(q * nb, nb)
            out = pl.ds(pl.multiple_of(q * ib, ib), ib)
            values = cols[pl.ds(at, nb)].astype(F32).reshape(nb * 32, 128)
            normed = layer_norm(values, gain).astype(F32).reshape(nb, 4, 8, 128)
            for c in range(4):
                nc = normed[:, c].reshape(ib, 128).astype(BF16)
                kbuf[c, out, :] = jnp.dot(nc, wre[1], preferred_element_type=F32).astype(BF16)
                qt = lax.dot_general(wre[0], nc, NT, preferred_element_type=F32)
                qbuf[c, q] = qt.astype(BF16)
                vt = lax.dot_general(wre[2], nc, NT, preferred_element_type=F32).astype(BF16)
                for pair in range(2):
                    vbuf[c, pair, :64, out] = vt[pair * 64 : pair * 64 + 64]
                gt = lax.dot_general(wre[3], nc, NT, preferred_element_type=F32)
                gbuf[c, q] = jax.nn.sigmoid(gt.astype(BF16).astype(F32))
            return carry

        lax.fori_loop(0, ny, chunk, 0)

    def repack(b):
        def line(q, carry):
            at = pl.ds(pl.multiple_of(q * ib, ib), ib)
            for a in range(2):
                g0 = gath[0, a, q, b].astype(F32)
                g1 = gath[1, a, q, b].astype(F32)
                for hh in range(2):
                    both = jnp.concatenate([g0[:, hh * 8 : hh * 8 + 8], g1[:, hh * 8 : hh * 8 + 8]], 1)
                    btab[a, at, hh * ib : (hh + 1) * ib] = both.reshape(ib, ib)
            return carry

        lax.fori_loop(0, ny, line, 0)

    qrow = lax.broadcasted_iota(jnp.int32, (128, ib), 0) // 32

    def attend(b, hf):
        at = pl.ds(pl.multiple_of(b * ib, ib), ib)
        blk = pl.ds(pl.multiple_of(b * nb, nb), nb)
        sub16 = pl.ds(pl.multiple_of(hf * 16, 16), 16)
        before = cols[blk, sub16].astype(F32)
        units = [(cc, pair) for cc in range(2) for pair in range(2)]
        scores = []
        for cc, pair in units:
            qt = qbuf[hf * 2 + cc, b]
            rhs = jnp.concatenate(
                [jnp.where(qrow == 2 * pair + hh, qt, jnp.zeros_like(qt)) for hh in range(2)], 1
            )
            s = jnp.dot(kbuf[hf * 2 + cc], rhs, preferred_element_type=F32)
            scores.append(s + btab[pair])
        tops = [jnp.max(s, 0, keepdims=True) for s in scores]
        probs = [
            jnp.exp2((s - top) * (SCALE * math.log2(math.e))).astype(BF16)
            for s, top in zip(scores, tops)
        ]
        outs = [
            jnp.dot(vbuf[hf * 2 + cc, pair], p, preferred_element_type=F32)
            for (cc, pair), p in zip(units, probs)
        ]
        after = []
        for cc in range(2):
            c = hf * 2 + cc
            att = []
            for pair in range(2):
                o = outs[2 * cc + pair]
                for hh in range(2):
                    lanes = slice(hh * ib, (hh + 1) * ib)
                    att.append(o[hh * 32 : hh * 32 + 32, lanes] / o[64:65, lanes])
            gated = (gbuf[c, b] * jnp.concatenate(att, 0)).astype(BF16)
            upd = lax.dot_general(gated, wre[4], TN, preferred_element_type=F32)
            after.append(before[:, cc * 8 : cc * 8 + 8] + upd.reshape(nb, 8, 128))
        ns[blk, sub16] = jnp.concatenate(after, 1).astype(BF16)
        for cc in range(2):
            flat = after[cc].reshape(ib, 128).astype(BF16)
            logits = lax.dot_general(wdist_ref[...], flat, NT, preferred_element_type=F32) + db
            own_log[b, hf, cc * bins : (cc + 1) * bins, :] = logits.astype(BF16)

    def forward(t):
        part = rows.at[head, pl.ds(((y + 2 * ny - t - 1) % ny) * nb, nb)]
        wait_bytes(part, rsem.at[OUT + t])
        to_other(part, part, FWD + t).start()

    project()

    def step(t, carry):
        b = (y + t + 1) % ny

        @pl.when(t < ny - 2)
        def _():
            after_y(t + 2)

        @pl.when(t < ny - 1)
        def _():
            after_x(t + 1)

        wait_bytes(gath.at[1 - core, :, :, b], rsem.at[BIAS_C + t])
        repack(b)

        def two(hf, c2):
            attend(b, hf)

            @pl.when(t == ny - 1)
            def _():
                part = pl.ds(pl.multiple_of(hf * 16, 16), 16)

                def send_half(j, c3):
                    target = b * nb + (me % nb + j) % nb
                    to_row(
                        ns.at[target, part], rows.at[head, me, part], OUT + ny - 1, target
                    ).start()
                    return c3

                lax.fori_loop(1, nb, send_half, 0)

            return c2

        lax.fori_loop(0, 2, two, 0)

        def send(j, c3):
            target = b * nb + (me % nb + j) % nb
            to_row(ns.at[target], rows.at[head, me], OUT + t, target).start()
            return c3

        lax.fori_loop(0, jnp.where(t == ny - 1, 0, nb), send, 0)

        @pl.when(t == ny - 1)
        def _():
            pltpu.make_async_copy(ns.at[me], rows.at[head, me], rsem.at[OUT + ny - 1]).start()

        to_other(own_log.at[b], logc.at[head, b], LOG).start()
        pltpu.make_async_copy(own_log.at[b], logc.at[head, b], rsem.at[X_IN]).start()

        @pl.when(t >= 1)
        def _():
            forward(t - 1)

        return carry

    lax.fori_loop(0, ny, step, 0)
    forward(ny - 1)
    for t in range(ny):
        part = rows.at[other, pl.ds(((y + 2 * ny - t - 1) % ny) * nb, nb)]
        wait_bytes(part, rsem.at[FWD + t])
    wait_bytes(logc.at[other], rsem.at[LOG])
    wait_bytes(logc.at[head], rsem.at[X_IN])

    wait_bytes(xs.at[pl.ds(0, nb - 1)], ssem.at[PEERS_IN])
    for d in range(1, ny):
        wait_bytes(xs.at[pl.ds(0, nb)], ssem.at[PEERS_IN + d])
    for t in range(ny - 1):
        wait_bytes(ns.at[pl.ds(0, nb)], ssem.at[OUT + t])
    wait_bytes(ns.at[pl.ds(0, nb - 1)], ssem.at[OUT + ny - 1])
    for t in range(ny):
        wait_bytes(ns.at[pl.ds(0, nb)], ssem.at[FWD + t])
    wait_bytes(own_log, ssem.at[LOG])
    wait_bytes(gath.at[0, 0, 0, :, pl.ds(0, nz - 1)], ssem.at[BIAS_Z])
    for t in range(ny):
        for d in range(1, ny):
            wait_bytes(gath.at[core, head, y, 0], ssem.at[BIAS_Y + t * (ny - 1) + d - 1])
        wait_bytes(gath.at[core, head, :, 0], ssem.at[BIAS_X + t])
        wait_bytes(gath.at[core, :, :, 0], ssem.at[BIAS_C + t])


def finish(nb, rows_ref, logc_ref, wdist_ref, dbias_ref, new_ref, dist_ref, turn):
    bins = wdist_ref.shape[0]
    bi = lax.broadcasted_iota(jnp.int32, (bins, bins), 0)
    bj = lax.broadcasted_iota(jnp.int32, (bins, bins), 1)
    db = jnp.sum(jnp.where(bi == bj, dbias_ref[...], 0.0), -1, keepdims=True)
    for a in range(2):
        for r in range(nb):
            turn[r * 64 + a * 32 : r * 64 + a * 32 + 32, :] = rows_ref[a, r].astype(F32)
    for kk in range(8):
        new = turn[pl.ds(kk, nb * 8, stride=8), :].astype(BF16)
        new_ref[kk] = new
        own = (lax.dot_general(wdist_ref[...], new, NT, preferred_element_type=F32) + db).astype(BF16)
        c = kk % 2
        mirrored = logc_ref[kk // 4, 0, (kk // 2) % 2, c * bins : (c + 1) * bins, :]
        dist_ref[kk] = (own.astype(F32) + mirrored.astype(F32)).astype(BF16)


def shards(
    pair_act,
    chain_id,
    residue_mask,
    norm_gain,
    w_proj,
    w_bias,
    chain_bias,
    w_out,
    w_dist,
    dist_bias,
):
    _, n, width = pair_act.shape
    nr = n // 8
    ny, nz = SHAPE[nr]
    bins = w_dist.shape[1]
    ib = n // ny
    nb = nr // ny
    vmem = pl.BlockSpec(memory_space=pltpu.VMEM)
    smem = pl.BlockSpec(memory_space=pltpu.SMEM)
    hbm = pl.BlockSpec(memory_space=pl.ANY)
    wdist_t = w_dist.T
    dbias = dist_bias.reshape(1, bins)
    rows, logc = pl.pallas_call(
        functools.partial(kernel, ny, nz),
        out_shape=(
            jax.ShapeDtypeStruct((2, nr, 32, width), BF16),
            jax.ShapeDtypeStruct((2, ny, 2, 2 * bins, ib), BF16),
        ),
        in_specs=[hbm, vmem, vmem, vmem, vmem, vmem, smem, vmem, vmem, vmem],
        out_specs=(hbm, hbm),
        scratch_shapes=[
            pltpu.VMEM((8, n, width), BF16),
            pltpu.VMEM((n * 8, width), F32),
            pltpu.VMEM((nr, 32, width), BF16),
            pltpu.VMEM((nr, 32, width), BF16),
            pltpu.VMEM((2, 2, ny, ny, nz, 16, ib), BF16),
            pltpu.VMEM((2, n, 2 * ib), F32),
            pltpu.VMEM((2, 8, n), F32),
            pltpu.VMEM((2 * width, 128), BF16),
            pltpu.VMEM((64, width), BF16),
            pltpu.VMEM((5, width, width), BF16),
            pltpu.VMEM((4, ny, width, ib), BF16),
            pltpu.VMEM((4, n, width), BF16),
            pltpu.VMEM((4, 2, 80, n), BF16),
            pltpu.VMEM((4, ny, width, ib), F32),
            pltpu.VMEM((nr, 32, width), BF16),
            pltpu.VMEM((ny, 2, 2 * bins, ib), BF16),
            pltpu.SemaphoreType.DMA((N_SEM,)),
            pltpu.SemaphoreType.DMA((N_SEM,)),
        ],
        compiler_params=pltpu.CompilerParams(
            collective_id=0, has_side_effects=True, vmem_limit_bytes=60 << 20
        ),
        name="triangle",
    )(
        pair_act,
        chain_id.reshape(1, n),
        residue_mask.reshape(1, n),
        norm_gain.reshape(1, width),
        w_proj.reshape(2 * width, 128),
        w_bias.T,
        chain_bias,
        w_out.reshape(64, width),
        wdist_t,
        dbias,
    )
    new, dist = pl.pallas_call(
        functools.partial(finish, nb),
        grid=(ny,),
        out_shape=(
            jax.ShapeDtypeStruct((8, n, width), BF16),
            jax.ShapeDtypeStruct((8, bins, n), BF16),
        ),
        in_specs=[
            pl.BlockSpec((2, nb, 32, width), lambda q: (0, q, 0, 0)),
            pl.BlockSpec((2, 1, 2, 2 * bins, ib), lambda q: (0, q, 0, 0, 0)),
            pl.BlockSpec((bins, width), lambda q: (0, 0)),
            pl.BlockSpec((1, bins), lambda q: (0, 0)),
        ],
        out_specs=(
            pl.BlockSpec((8, ib, width), lambda q: (0, q, 0)),
            pl.BlockSpec((8, bins, ib), lambda q: (0, 0, q)),
        ),
        scratch_shapes=[pltpu.VMEM((nb * 64, width), F32)],
        compiler_params=pltpu.CompilerParams(vmem_limit_bytes=62 << 20),
        name="finish",
    )(rows, logc, wdist_t, dbias)
    return new, jnp.transpose(dist, (0, 2, 1))


def solution(mesh):
    in_specs = (
        P(("dp", "row"), None, None),
        P("dp"),
        P("dp"),
        P(),
        P(None, "head", None),
        P(None, "head"),
        P(None, "head"),
        P("head", None, None),
        P(),
        P(),
    )
    out_specs = (P(("dp", "row"), None, None), P(("dp", "row"), None, None))
    return jax.shard_map(shards, mesh=mesh, in_specs=in_specs, out_specs=out_specs, check_vma=False)
```

```python
import functools
import math

import jax
import jax.numpy as jnp
from jax import lax
from jax.experimental import pallas as pl
from jax.experimental.pallas import tpu as pltpu
from jax.sharding import PartitionSpec as P

MESH = pl.DeviceIdType.MESH
F32 = jnp.float32
BF16 = jnp.bfloat16
NT = (((1,), (1,)), ((), ()))
TN = (((0,), (0,)), ((), ()))
SCALE = 32.0**-0.5
SHAPE = {64: (4, 8), 8: (2, 2)}
PEERS_IN, BIAS_Z, BIAS_Y, BIAS_X, BIAS_C, W_P, W_O, LOG, X_IN, OUT, FWD = 0, 4, 5, 17, 21, 25, 26, 27, 28, 29, 34
N_SEM = 38


def layer_norm(values, gain):
    center = jnp.mean(values, -1, keepdims=True)
    centered = values - center
    variance = jnp.mean(centered * centered, -1, keepdims=True)
    return (centered * lax.rsqrt(variance + 1e-05) * gain).astype(BF16)


def kernel(
    ny,
    nz,
    x_ref,
    chain_ref,
    mask_ref,
    gain_ref,
    wproj_ref,
    wbias_ref,
    cbias_ref,
    wout_ref,
    wdist_ref,
    dbias_ref,
    rows,
    logc,
    xbuf,
    turn,
    xs,
    cols,
    gath,
    btab,
    bsc,
    wpg,
    wog,
    wre,
    qbuf,
    kbuf,
    vbuf,
    gbuf,
    ns,
    own_log,
    ssem,
    rsem,
    ready,
):
    nr = ny * nz * 2
    n = nr * 8
    ib = n // ny
    nb = nr // ny
    bins = wdist_ref.shape[0]
    head = lax.axis_index("head")
    me = lax.axis_index("row")
    core = me % 2
    z = (me // 2) % nz
    y = me // (2 * nz)
    other = 1 - head

    def row_of(yy, zz, cc):
        return (yy * nz + zz) * 2 + cc

    def peer(idx):
        t = idx % nz
        rest = idx // nz
        sign = 2 * (t % 2) - 1
        dz = (sign * ((t + 1) // 2) + nz) % nz
        return row_of((y + rest // 2) % ny, (z + dz) % nz, (core + rest % 2) % 2)

    def to_row(src, dst, sem, target):
        return pltpu.make_async_remote_copy(
            src_ref=src,
            dst_ref=dst,
            send_sem=ssem.at[sem],
            recv_sem=rsem.at[sem],
            device_id={"row": target},
            device_id_type=MESH,
        )

    def to_other(src, dst, sem):
        return pltpu.make_async_remote_copy(
            src_ref=src,
            dst_ref=dst,
            send_sem=ssem.at[sem],
            recv_sem=rsem.at[sem],
            device_id={"head": other},
            device_id_type=MESH,
        )

    def wait_bytes(ref, sem):
        pltpu.make_async_copy(ref, ref, sem).wait()

    pltpu.make_async_copy(x_ref, xbuf, rsem.at[X_IN]).start()

    barrier = pltpu.get_barrier_semaphore()

    near = [row_of(y, (z + d) % nz, core) for d in range(1, nz)]
    cross = [row_of((y + i // 2) % ny, z, (core + i % 2) % 2) for i in range(1, 2 * ny)]
    for p in near + cross:
        pl.semaphore_signal(barrier, inc=1, device_id={"row": p}, device_id_type=MESH)
    pl.semaphore_signal(barrier, inc=1, device_id={"head": other}, device_id_type=MESH)

    gain = gain_ref[...]

    pltpu.make_async_copy(x_ref, xbuf, rsem.at[X_IN]).wait()

    def prepare(kk, carry):
        xk = xbuf[kk].astype(F32)
        turn[pl.ds(kk, n, stride=8), :] = xk
        nk = layer_norm(xk, gain)
        bk = lax.dot_general(wbias_ref[...], nk, NT, preferred_element_type=F32)
        bsc[0, pl.ds(kk, 1), :] = bk[0:1]
        bsc[1, pl.ds(kk, 1), :] = bk[1:2]
        return carry

    lax.fori_loop(0, 8, prepare, 0)

    pl.semaphore_wait(barrier, nz + 2 * ny - 1)
    for p in cross:
        pl.semaphore_signal(ready, inc=1, device_id={"row": p}, device_id_type=MESH)
    def pick(i, carry):
        for j in range(nb // 2):
            r = i * (nb // 2) + j
            xs[r] = turn[pl.ds(pl.multiple_of(r * 64 + head * 32, 32), 32), :].astype(BF16)
        return carry

    lax.fori_loop(0, 2 * ny, pick, 0)

    ids = chain_ref[...]
    lane = lax.broadcasted_iota(jnp.int32, (8, n), 1)
    sub = lax.broadcasted_iota(jnp.int32, (8, n), 0)
    mine = lane == sub + me * 8
    my_ids = jnp.sum(jnp.where(mine, ids, 0), -1, keepdims=True)
    my_mask = jnp.sum(jnp.where(mine, mask_ref[...], 0), -1, keepdims=True)
    mask_term = (my_mask.astype(F32) - 1.0) * 1000000000.0
    same = my_ids == ids
    blocks = []
    for hh in range(2):
        chain_term = jnp.where(same, cbias_ref[1, hh], cbias_ref[0, hh])
        blocks.append((bsc[hh] + chain_term + mask_term) * (1.0 / SCALE))
    block = jnp.concatenate(blocks, 0).astype(BF16)
    for b in range(ny):
        gath[core, head, y, b, z] = block[:, b * ib : (b + 1) * ib]

    pl.semaphore_wait(ready, 2 * ny - 1)

    def send_cols(i, carry):
        q = peer(i)
        to_row(xs.at[q], cols.at[me], PEERS_IN + i // nb, q).start()
        return carry

    def bias_z():
        part = gath.at[core, head, y, :, z]
        for d in range(1, nz):
            to_row(part, part, BIAS_Z, row_of(y, (z + d) % nz, core)).start()

    def bias_y(t):
        for d in range(1, ny):
            part = gath.at[core, head, y, (y + d + t + 1) % ny]
            to_row(part, part, BIAS_Y + t * (ny - 1) + d - 1, row_of((y + d) % ny, z, core)).start()

    sib = row_of(y, z, 1 - core)

    def pass_on(line, t):
        part = gath.at[core, head, line, (y + t + 1) % ny]
        to_other(part, part, BIAS_X + t).start()
        to_row(part, part, BIAS_C + t, sib).start()

    def after_y(t):
        for d in range(1, ny):
            line = (y + ny - d) % ny
            wait_bytes(
                gath.at[core, head, line, (y + t + 1) % ny], rsem.at[BIAS_Y + t * (ny - 1) + d - 1]
            )
            pass_on(line, t)

    def after_x(t):
        part = gath.at[core, other, :, (y + t + 1) % ny]
        wait_bytes(part, rsem.at[BIAS_X + t])
        to_row(part, part, BIAS_C + t, sib).start()

    bias_z()
    w_p = to_other(wproj_ref, wpg, W_P)
    w_p.start()
    w_o = to_other(wout_ref, wog, W_O)
    w_o.start()
    lax.fori_loop(1, nr, send_cols, 0)
    pltpu.make_async_copy(xs.at[me], cols.at[me], rsem.at[PEERS_IN]).start()

    li = lax.broadcasted_iota(jnp.int32, (128, 128), 0)
    mi = lax.broadcasted_iota(jnp.int32, (128, 128), 1)
    shift = li - mi
    mh = mi // 32
    ri = lax.broadcasted_iota(jnp.int32, (128, 256), 0) * 2
    rj = lax.broadcasted_iota(jnp.int32, (128, 256), 1)

    def arrange(which, ref):
        total = [jnp.zeros((128, 128), F32) for _ in range(4)]
        for hh in range(2):
            h = 2 * which + hh
            split = jnp.where(rj == ri + hh, 1.0, 0.0).astype(BF16)
            w = jnp.dot(split, ref[...], preferred_element_type=F32).astype(BF16)
            for t in range(4):
                pick = jnp.where((shift == 32 * (t - h)) & (mh == h), 1.0, 0.0).astype(BF16)
                total[t] += jnp.dot(w, pick, preferred_element_type=F32)
        return total

    mine_w = arrange(head, wproj_ref)
    for t in range(4):
        wre[t] = mine_w[t].astype(BF16)
    wre[4, pl.ds(pl.multiple_of(head * 64, 64), 64), :] = wout_ref[...]
    bi = lax.broadcasted_iota(jnp.int32, (bins, bins), 0)
    bj = lax.broadcasted_iota(jnp.int32, (bins, bins), 1)
    db = jnp.sum(jnp.where(bi == bj, dbias_ref[...], 0.0), -1, keepdims=True)
    for c in range(4):
        for pair in range(2):
            vbuf[c, pair, 64:, :] = jnp.ones((16, n), BF16)

    wait_bytes(gath.at[0, 0, 0, :, pl.ds(0, nz - 1)], rsem.at[BIAS_Z])
    for t in range(ny):
        bias_y(t)
    for t in range(ny):
        pass_on(y, t)
    w_p.wait()
    w_o.wait()
    their_w = arrange(other, wpg)
    for t in range(4):
        full = wre[t].astype(F32) + their_w[t]
        wre[t] = (full if t == 1 else jnp.transpose(full)).astype(BF16)
    wre[4, pl.ds(pl.multiple_of(other * 64, 64), 64), :] = wog[...]
    after_y(0)
    after_y(1)
    after_x(0)

    def project():
        def chunk(d, carry):
            q = (y + ny - d) % ny
            wait_bytes(cols.at[pl.ds(q * nb, nb)], rsem.at[PEERS_IN + d])
            at = pl.multiple_of(q * nb, nb)
            out = pl.ds(pl.multiple_of(q * ib, ib), ib)
            values = cols[pl.ds(at, nb)].astype(F32).reshape(nb * 32, 128)
            normed = layer_norm(values, gain).astype(F32).reshape(nb, 4, 8, 128)
            for c in range(4):
                nc = normed[:, c].reshape(ib, 128).astype(BF16)
                kbuf[c, out, :] = jnp.dot(nc, wre[1], preferred_element_type=F32).astype(BF16)
                qt = lax.dot_general(wre[0], nc, NT, preferred_element_type=F32)
                qbuf[c, q] = qt.astype(BF16)
                vt = lax.dot_general(wre[2], nc, NT, preferred_element_type=F32).astype(BF16)
                for pair in range(2):
                    vbuf[c, pair, :64, out] = vt[pair * 64 : pair * 64 + 64]
                gt = lax.dot_general(wre[3], nc, NT, preferred_element_type=F32)
                gbuf[c, q] = jax.nn.sigmoid(gt.astype(BF16).astype(F32))
            return carry

        lax.fori_loop(0, ny, chunk, 0)

    def repack(b):
        def line(q, carry):
            at = pl.ds(pl.multiple_of(q * ib, ib), ib)
            for a in range(2):
                g0 = gath[0, a, q, b].astype(F32)
                g1 = gath[1, a, q, b].astype(F32)
                for hh in range(2):
                    both = jnp.concatenate([g0[:, hh * 8 : hh * 8 + 8], g1[:, hh * 8 : hh * 8 + 8]], 1)
                    btab[a, at, hh * ib : (hh + 1) * ib] = both.reshape(ib, ib)
            return carry

        lax.fori_loop(0, ny, line, 0)

    qrow = lax.broadcasted_iota(jnp.int32, (128, ib), 0) // 32

    def attend(b, hf):
        at = pl.ds(pl.multiple_of(b * ib, ib), ib)
        blk = pl.ds(pl.multiple_of(b * nb, nb), nb)
        sub16 = pl.ds(pl.multiple_of(hf * 16, 16), 16)
        before = cols[blk, sub16].astype(F32)
        units = [(cc, pair) for cc in range(2) for pair in range(2)]
        scores = []
        for cc, pair in units:
            qt = qbuf[hf * 2 + cc, b]
            rhs = jnp.concatenate(
                [jnp.where(qrow == 2 * pair + hh, qt, jnp.zeros_like(qt)) for hh in range(2)], 1
            )
            s = jnp.dot(kbuf[hf * 2 + cc], rhs, preferred_element_type=F32)
            scores.append(s + btab[pair])
        tops = [jnp.max(s, 0, keepdims=True) for s in scores]
        probs = [
            jnp.exp2((s - top) * (SCALE * math.log2(math.e))).astype(BF16)
            for s, top in zip(scores, tops)
        ]
        outs = [
            jnp.dot(vbuf[hf * 2 + cc, pair], p, preferred_element_type=F32)
            for (cc, pair), p in zip(units, probs)
        ]
        after = []
        for cc in range(2):
            c = hf * 2 + cc
            att = []
            for pair in range(2):
                o = outs[2 * cc + pair]
                for hh in range(2):
                    lanes = slice(hh * ib, (hh + 1) * ib)
                    att.append(o[hh * 32 : hh * 32 + 32, lanes] / o[64:65, lanes])
            gated = (gbuf[c, b] * jnp.concatenate(att, 0)).astype(BF16)
            upd = lax.dot_general(gated, wre[4], TN, preferred_element_type=F32)
            after.append(before[:, cc * 8 : cc * 8 + 8] + upd.reshape(nb, 8, 128))
        ns[blk, sub16] = jnp.concatenate(after, 1).astype(BF16)
        for cc in range(2):
            flat = after[cc].reshape(ib, 128).astype(BF16)
            logits = lax.dot_general(wdist_ref[...], flat, NT, preferred_element_type=F32) + db
            own_log[b, hf, cc * bins : (cc + 1) * bins, :] = logits.astype(BF16)

    def forward(t):
        part = rows.at[head, pl.ds(((y + 2 * ny - t - 1) % ny) * nb, nb)]
        wait_bytes(part, rsem.at[OUT + t])
        to_other(part, part, FWD + t).start()

    project()

    def step(t, carry):
        b = (y + t + 1) % ny

        wait_bytes(gath.at[1 - core, :, :, b], rsem.at[BIAS_C + t])
        repack(b)

        def two(hf, c2):
            @pl.when((hf == 1) & (t < ny - 2))
            def _():
                after_y(t + 2)

            @pl.when((hf == 1) & (t < ny - 1))
            def _():
                after_x(t + 1)

            attend(b, hf)

            @pl.when(t == ny - 1)
            def _():
                part = pl.ds(pl.multiple_of(hf * 16, 16), 16)

                def send_half(j, c3):
                    target = b * nb + (me % nb + j) % nb
                    to_row(
                        ns.at[target, part], rows.at[head, me, part], OUT + ny - 1 + hf, target
                    ).start()
                    return c3

                lax.fori_loop(1, nb, send_half, 0)

            return c2

        lax.fori_loop(0, 2, two, 0)

        def send(j, c3):
            target = b * nb + (me % nb + j) % nb
            to_row(ns.at[target], rows.at[head, me], OUT + t, target).start()
            return c3

        lax.fori_loop(0, jnp.where(t == ny - 1, 0, nb), send, 0)

        @pl.when(t == ny - 1)
        def _():
            for hf in range(2):
                part = pl.ds(hf * 16, 16)
                pltpu.make_async_copy(
                    ns.at[me, part], rows.at[head, me, part], rsem.at[OUT + ny - 1 + hf]
                ).start()

        to_other(own_log.at[b], logc.at[head, b], LOG).start()
        pltpu.make_async_copy(own_log.at[b], logc.at[head, b], rsem.at[X_IN]).start()

        @pl.when(t >= 1)
        def _():
            forward(t - 1)

        return carry

    lax.fori_loop(0, ny, step, 0)
    for hf in range(2):
        part = rows.at[head, pl.ds(y * nb, nb), pl.ds(hf * 16, 16)]
        wait_bytes(part, rsem.at[OUT + ny - 1 + hf])
        to_other(part, part, FWD + ny - 1).start()
    for t in range(ny):
        part = rows.at[other, pl.ds(((y + 2 * ny - t - 1) % ny) * nb, nb)]
        wait_bytes(part, rsem.at[FWD + t])
    wait_bytes(logc.at[other], rsem.at[LOG])
    wait_bytes(logc.at[head], rsem.at[X_IN])

    wait_bytes(xs.at[pl.ds(0, nb - 1)], ssem.at[PEERS_IN])
    for d in range(1, ny):
        wait_bytes(xs.at[pl.ds(0, nb)], ssem.at[PEERS_IN + d])
    for t in range(ny - 1):
        wait_bytes(ns.at[pl.ds(0, nb)], ssem.at[OUT + t])
    for hf in range(2):
        wait_bytes(ns.at[pl.ds(0, nb - 1), pl.ds(0, 16)], ssem.at[OUT + ny - 1 + hf])
    for t in range(ny):
        wait_bytes(ns.at[pl.ds(0, nb)], ssem.at[FWD + t])
    wait_bytes(own_log, ssem.at[LOG])
    wait_bytes(gath.at[0, 0, 0, :, pl.ds(0, nz - 1)], ssem.at[BIAS_Z])
    for t in range(ny):
        for d in range(1, ny):
            wait_bytes(gath.at[core, head, y, 0], ssem.at[BIAS_Y + t * (ny - 1) + d - 1])
        wait_bytes(gath.at[core, head, :, 0], ssem.at[BIAS_X + t])
        wait_bytes(gath.at[core, :, :, 0], ssem.at[BIAS_C + t])


def finish(nb, rows_ref, logc_ref, wdist_ref, dbias_ref, new_ref, dist_ref, turn):
    bins = wdist_ref.shape[0]
    bi = lax.broadcasted_iota(jnp.int32, (bins, bins), 0)
    bj = lax.broadcasted_iota(jnp.int32, (bins, bins), 1)
    db = jnp.sum(jnp.where(bi == bj, dbias_ref[...], 0.0), -1, keepdims=True)
    for a in range(2):
        for r in range(nb):
            turn[r * 64 + a * 32 : r * 64 + a * 32 + 32, :] = rows_ref[a, r].astype(F32)
    news = [turn[pl.ds(kk, nb * 8, stride=8), :].astype(BF16) for kk in range(8)]
    flat = jnp.concatenate(news, 0)
    own = (lax.dot_general(wdist_ref[...], flat, NT, preferred_element_type=F32) + db).astype(BF16)
    own = own.astype(F32)
    for kk in range(8):
        new_ref[kk] = news[kk]
        c = kk % 2
        mirrored = logc_ref[kk // 4, 0, (kk // 2) % 2, c * bins : (c + 1) * bins, :]
        mine = own[:, kk * nb * 8 : (kk + 1) * nb * 8]
        dist_ref[kk] = (mine + mirrored.astype(F32)).astype(BF16)


def shards(
    pair_act,
    chain_id,
    residue_mask,
    norm_gain,
    w_proj,
    w_bias,
    chain_bias,
    w_out,
    w_dist,
    dist_bias,
):
    _, n, width = pair_act.shape
    nr = n // 8
    ny, nz = SHAPE[nr]
    bins = w_dist.shape[1]
    ib = n // ny
    nb = nr // ny
    vmem = pl.BlockSpec(memory_space=pltpu.VMEM)
    smem = pl.BlockSpec(memory_space=pltpu.SMEM)
    hbm = pl.BlockSpec(memory_space=pl.ANY)
    wdist_t = w_dist.T
    dbias = dist_bias.reshape(1, bins)
    rows, logc = pl.pallas_call(
        functools.partial(kernel, ny, nz),
        out_shape=(
            jax.ShapeDtypeStruct((2, nr, 32, width), BF16),
            jax.ShapeDtypeStruct((2, ny, 2, 2 * bins, ib), BF16),
        ),
        in_specs=[hbm, vmem, vmem, vmem, vmem, vmem, smem, vmem, vmem, vmem],
        out_specs=(hbm, hbm),
        scratch_shapes=[
            pltpu.VMEM((8, n, width), BF16),
            pltpu.VMEM((n * 8, width), F32),
            pltpu.VMEM((nr, 32, width), BF16),
            pltpu.VMEM((nr, 32, width), BF16),
            pltpu.VMEM((2, 2, ny, ny, nz, 16, ib), BF16),
            pltpu.VMEM((2, n, 2 * ib), F32),
            pltpu.VMEM((2, 8, n), F32),
            pltpu.VMEM((2 * width, 128), BF16),
            pltpu.VMEM((64, width), BF16),
            pltpu.VMEM((5, width, width), BF16),
            pltpu.VMEM((4, ny, width, ib), BF16),
            pltpu.VMEM((4, n, width), BF16),
            pltpu.VMEM((4, 2, 80, n), BF16),
            pltpu.VMEM((4, ny, width, ib), F32),
            pltpu.VMEM((nr, 32, width), BF16),
            pltpu.VMEM((ny, 2, 2 * bins, ib), BF16),
            pltpu.SemaphoreType.DMA((N_SEM,)),
            pltpu.SemaphoreType.DMA((N_SEM,)),
            pltpu.SemaphoreType.REGULAR,
        ],
        compiler_params=pltpu.CompilerParams(
            collective_id=0, has_side_effects=True, vmem_limit_bytes=60 << 20
        ),
        name="triangle",
    )(
        pair_act,
        chain_id.reshape(1, n),
        residue_mask.reshape(1, n),
        norm_gain.reshape(1, width),
        w_proj.reshape(2 * width, 128),
        w_bias.T,
        chain_bias,
        w_out.reshape(64, width),
        wdist_t,
        dbias,
    )
    new, dist = pl.pallas_call(
        functools.partial(finish, nb),
        grid=(ny,),
        out_shape=(
            jax.ShapeDtypeStruct((8, n, width), BF16),
            jax.ShapeDtypeStruct((8, bins, n), BF16),
        ),
        in_specs=[
            pl.BlockSpec((2, nb, 32, width), lambda q: (0, q, 0, 0)),
            pl.BlockSpec((2, 1, 2, 2 * bins, ib), lambda q: (0, q, 0, 0, 0)),
            pl.BlockSpec((bins, width), lambda q: (0, 0)),
            pl.BlockSpec((1, bins), lambda q: (0, 0)),
        ],
        out_specs=(
            pl.BlockSpec((8, ib, width), lambda q: (0, q, 0)),
            pl.BlockSpec((8, bins, ib), lambda q: (0, 0, q)),
        ),
        scratch_shapes=[pltpu.VMEM((nb * 64, width), F32)],
        compiler_params=pltpu.CompilerParams(vmem_limit_bytes=62 << 20),
        name="finish",
    )(rows, logc, wdist_t, dbias)
    return new, jnp.transpose(dist, (0, 2, 1))


def solution(mesh):
    in_specs = (
        P(("dp", "row"), None, None),
        P("dp"),
        P("dp"),
        P(),
        P(None, "head", None),
        P(None, "head"),
        P(None, "head"),
        P("head", None, None),
        P(),
        P(),
    )
    out_specs = (P(("dp", "row"), None, None), P(("dp", "row"), None, None))
    return jax.shard_map(shards, mesh=mesh, in_specs=in_specs, out_specs=out_specs, check_vma=False)
```

```python
import functools
import math

import jax
import jax.numpy as jnp
from jax import lax
from jax.experimental import pallas as pl
from jax.experimental.pallas import tpu as pltpu
from jax.sharding import PartitionSpec as P

MESH = pl.DeviceIdType.MESH
F32 = jnp.float32
BF16 = jnp.bfloat16
NT = (((1,), (1,)), ((), ()))
TN = (((0,), (0,)), ((), ()))
SCALE = 32.0**-0.5
SHAPE = {64: (4, 8), 8: (2, 2)}
PEERS_IN, BIAS_Z, BIAS_Y, BIAS_X, BIAS_C, W_P, W_O, LOG, X_IN, OUT, FWD = 0, 4, 5, 17, 21, 25, 26, 27, 28, 29, 34
N_SEM = 38


def layer_norm(values, gain):
    center = jnp.mean(values, -1, keepdims=True)
    centered = values - center
    variance = jnp.mean(centered * centered, -1, keepdims=True)
    return (centered * lax.rsqrt(variance + 1e-05) * gain).astype(BF16)


def kernel(
    ny,
    nz,
    x_ref,
    chain_ref,
    mask_ref,
    gain_ref,
    wproj_ref,
    wbias_ref,
    cbias_ref,
    wout_ref,
    wdist_ref,
    dbias_ref,
    rows,
    logc,
    xbuf,
    turn,
    xs,
    cols,
    gath,
    btab,
    bsc,
    wpg,
    wog,
    wre,
    qbuf,
    kbuf,
    vbuf,
    gbuf,
    ns,
    own_log,
    ssem,
    rsem,
    ready,
):
    nr = ny * nz * 2
    n = nr * 8
    ib = n // ny
    nb = nr // ny
    bins = wdist_ref.shape[0]
    head = lax.axis_index("head")
    me = lax.axis_index("row")
    core = me % 2
    z = (me // 2) % nz
    y = me // (2 * nz)
    other = 1 - head

    def row_of(yy, zz, cc):
        return (yy * nz + zz) * 2 + cc

    def peer(idx):
        t = idx % nz
        rest = idx // nz
        sign = 2 * (t % 2) - 1
        dz = (sign * ((t + 1) // 2) + nz) % nz
        return row_of((y + rest // 2) % ny, (z + dz) % nz, (core + rest % 2) % 2)

    def to_row(src, dst, sem, target):
        return pltpu.make_async_remote_copy(
            src_ref=src,
            dst_ref=dst,
            send_sem=ssem.at[sem],
            recv_sem=rsem.at[sem],
            device_id={"row": target},
            device_id_type=MESH,
        )

    def to_other(src, dst, sem):
        return pltpu.make_async_remote_copy(
            src_ref=src,
            dst_ref=dst,
            send_sem=ssem.at[sem],
            recv_sem=rsem.at[sem],
            device_id={"head": other},
            device_id_type=MESH,
        )

    def wait_bytes(ref, sem):
        pltpu.make_async_copy(ref, ref, sem).wait()

    pltpu.make_async_copy(x_ref, xbuf, rsem.at[X_IN]).start()

    barrier = pltpu.get_barrier_semaphore()

    near = [row_of(y, (z + d) % nz, core) for d in range(1, nz)]
    cross = [row_of((y + i // 2) % ny, z, (core + i % 2) % 2) for i in range(1, 2 * ny)]
    for p in near + cross:
        pl.semaphore_signal(barrier, inc=1, device_id={"row": p}, device_id_type=MESH)
    pl.semaphore_signal(barrier, inc=1, device_id={"head": other}, device_id_type=MESH)

    gain = gain_ref[...]

    pltpu.make_async_copy(x_ref, xbuf, rsem.at[X_IN]).wait()

    def prepare(kk, carry):
        xk = xbuf[kk].astype(F32)
        turn[pl.ds(kk, n, stride=8), :] = xk
        nk = layer_norm(xk, gain)
        bk = lax.dot_general(wbias_ref[...], nk, NT, preferred_element_type=F32)
        bsc[0, pl.ds(kk, 1), :] = bk[0:1]
        bsc[1, pl.ds(kk, 1), :] = bk[1:2]
        return carry

    lax.fori_loop(0, 8, prepare, 0)

    pl.semaphore_wait(barrier, nz + 2 * ny - 1)
    for p in cross:
        pl.semaphore_signal(ready, inc=1, device_id={"row": p}, device_id_type=MESH)
    def pick(i, carry):
        for j in range(nb // 2):
            r = i * (nb // 2) + j
            xs[r] = turn[pl.ds(pl.multiple_of(r * 64 + head * 32, 32), 32), :].astype(BF16)
        return carry

    lax.fori_loop(0, 2 * ny, pick, 0)

    ids = chain_ref[...]
    lane = lax.broadcasted_iota(jnp.int32, (8, n), 1)
    sub = lax.broadcasted_iota(jnp.int32, (8, n), 0)
    mine = lane == sub + me * 8
    my_ids = jnp.sum(jnp.where(mine, ids, 0), -1, keepdims=True)
    my_mask = jnp.sum(jnp.where(mine, mask_ref[...], 0), -1, keepdims=True)
    mask_term = (my_mask.astype(F32) - 1.0) * 1000000000.0
    same = my_ids == ids
    blocks = []
    for hh in range(2):
        chain_term = jnp.where(same, cbias_ref[1, hh], cbias_ref[0, hh])
        blocks.append((bsc[hh] + chain_term + mask_term) * (1.0 / SCALE))
    block = jnp.concatenate(blocks, 0).astype(BF16)
    for b in range(ny):
        gath[core, head, y, b, z] = block[:, b * ib : (b + 1) * ib]

    pl.semaphore_wait(ready, 2 * ny - 1)

    def send_cols(i, carry):
        q = peer(i)
        to_row(xs.at[q], cols.at[me], PEERS_IN + i // nb, q).start()
        return carry

    def bias_z():
        part = gath.at[core, head, y, :, z]
        for d in range(1, nz):
            to_row(part, part, BIAS_Z, row_of(y, (z + d) % nz, core)).start()

    def bias_y(t):
        for d in range(1, ny):
            part = gath.at[core, head, y, (y + d + t + 1) % ny]
            to_row(part, part, BIAS_Y + t * (ny - 1) + d - 1, row_of((y + d) % ny, z, core)).start()

    sib = row_of(y, z, 1 - core)

    def pass_on(line, t):
        part = gath.at[core, head, line, (y + t + 1) % ny]
        to_other(part, part, BIAS_X + t).start()
        to_row(part, part, BIAS_C + t, sib).start()

    def after_y(t):
        for d in range(1, ny):
            line = (y + ny - d) % ny
            wait_bytes(
                gath.at[core, head, line, (y + t + 1) % ny], rsem.at[BIAS_Y + t * (ny - 1) + d - 1]
            )
            pass_on(line, t)

    def after_x(t):
        part = gath.at[core, other, :, (y + t + 1) % ny]
        wait_bytes(part, rsem.at[BIAS_X + t])
        to_row(part, part, BIAS_C + t, sib).start()

    bias_z()
    w_p = to_other(wproj_ref, wpg, W_P)
    w_p.start()
    w_o = to_other(wout_ref, wog, W_O)
    w_o.start()
    lax.fori_loop(1, nr, send_cols, 0)
    pltpu.make_async_copy(xs.at[me], cols.at[me], rsem.at[PEERS_IN]).start()

    li = lax.broadcasted_iota(jnp.int32, (128, 128), 0)
    mi = lax.broadcasted_iota(jnp.int32, (128, 128), 1)
    shift = li - mi
    mh = mi // 32
    ri = lax.broadcasted_iota(jnp.int32, (128, 256), 0) * 2
    rj = lax.broadcasted_iota(jnp.int32, (128, 256), 1)

    def arrange(which, ref):
        total = [jnp.zeros((128, 128), F32) for _ in range(4)]
        for hh in range(2):
            h = 2 * which + hh
            split = jnp.where(rj == ri + hh, 1.0, 0.0).astype(BF16)
            w = jnp.dot(split, ref[...], preferred_element_type=F32).astype(BF16)
            for t in range(4):
                pick = jnp.where((shift == 32 * (t - h)) & (mh == h), 1.0, 0.0).astype(BF16)
                total[t] += jnp.dot(w, pick, preferred_element_type=F32)
        return total

    mine_w = arrange(head, wproj_ref)
    for t in range(4):
        wre[t] = mine_w[t].astype(BF16)
    wre[4, pl.ds(pl.multiple_of(head * 64, 64), 64), :] = wout_ref[...]
    bi = lax.broadcasted_iota(jnp.int32, (bins, bins), 0)
    bj = lax.broadcasted_iota(jnp.int32, (bins, bins), 1)
    db = jnp.sum(jnp.where(bi == bj, dbias_ref[...], 0.0), -1, keepdims=True)
    for c in range(4):
        for pair in range(2):
            vbuf[c, pair, 64:, :] = jnp.ones((16, n), BF16)

    wait_bytes(gath.at[0, 0, 0, :, pl.ds(0, nz - 1)], rsem.at[BIAS_Z])
    for t in range(ny):
        bias_y(t)
    for t in range(ny):
        pass_on(y, t)
    w_p.wait()
    w_o.wait()
    their_w = arrange(other, wpg)
    for t in range(4):
        full = wre[t].astype(F32) + their_w[t]
        wre[t] = (full if t == 1 else jnp.transpose(full)).astype(BF16)
    wre[4, pl.ds(pl.multiple_of(other * 64, 64), 64), :] = wog[...]
    after_y(0)
    after_y(1)
    after_x(0)

    def project():
        def chunk(d, carry):
            q = (y + ny - d) % ny
            wait_bytes(cols.at[pl.ds(q * nb, nb)], rsem.at[PEERS_IN + d])
            at = pl.multiple_of(q * nb, nb)
            out = pl.ds(pl.multiple_of(q * ib, ib), ib)
            values = cols[pl.ds(at, nb)].astype(F32).reshape(nb * 32, 128)
            normed = layer_norm(values, gain).astype(F32).reshape(nb, 4, 8, 128)
            for c in range(4):
                nc = normed[:, c].reshape(ib, 128).astype(BF16)
                kbuf[c, out, :] = jnp.dot(nc, wre[1], preferred_element_type=F32).astype(BF16)
                qt = lax.dot_general(wre[0], nc, NT, preferred_element_type=F32)
                qbuf[c, q] = qt.astype(BF16)
                vt = lax.dot_general(wre[2], nc, NT, preferred_element_type=F32).astype(BF16)
                for pair in range(2):
                    vbuf[c, pair, :64, out] = vt[pair * 64 : pair * 64 + 64]
                gt = lax.dot_general(wre[3], nc, NT, preferred_element_type=F32)
                gbuf[c, q] = jax.nn.sigmoid(gt.astype(BF16).astype(F32))
            return carry

        lax.fori_loop(0, ny, chunk, 0)

    def repack(b):
        def line(q, carry):
            at = pl.ds(pl.multiple_of(q * ib, ib), ib)
            for a in range(2):
                g0 = gath[0, a, q, b].astype(F32)
                g1 = gath[1, a, q, b].astype(F32)
                for hh in range(2):
                    both = jnp.concatenate([g0[:, hh * 8 : hh * 8 + 8], g1[:, hh * 8 : hh * 8 + 8]], 1)
                    btab[a, at, hh * ib : (hh + 1) * ib] = both.reshape(ib, ib)
            return carry

        lax.fori_loop(0, ny, line, 0)

    qrow = lax.broadcasted_iota(jnp.int32, (128, ib), 0) // 32

    def attend(b, hf):
        at = pl.ds(pl.multiple_of(b * ib, ib), ib)
        blk = pl.ds(pl.multiple_of(b * nb, nb), nb)
        sub16 = pl.ds(pl.multiple_of(hf * 16, 16), 16)
        before = cols[blk, sub16].astype(F32)
        units = [(cc, pair) for cc in range(2) for pair in range(2)]
        scores = []
        for cc, pair in units:
            qt = qbuf[hf * 2 + cc, b]
            rhs = jnp.concatenate(
                [jnp.where(qrow == 2 * pair + hh, qt, jnp.zeros_like(qt)) for hh in range(2)], 1
            )
            s = jnp.dot(kbuf[hf * 2 + cc], rhs, preferred_element_type=F32)
            scores.append(s + btab[pair])
        tops = [jnp.max(s, 0, keepdims=True) for s in scores]
        probs = [
            jnp.exp2((s - top) * (SCALE * math.log2(math.e))).astype(BF16)
            for s, top in zip(scores, tops)
        ]
        outs = [
            jnp.dot(vbuf[hf * 2 + cc, pair], p, preferred_element_type=F32)
            for (cc, pair), p in zip(units, probs)
        ]
        after = []
        for cc in range(2):
            c = hf * 2 + cc
            att = []
            for pair in range(2):
                o = outs[2 * cc + pair]
                for hh in range(2):
                    lanes = slice(hh * ib, (hh + 1) * ib)
                    att.append(o[hh * 32 : hh * 32 + 32, lanes] / o[64:65, lanes])
            gated = (gbuf[c, b] * jnp.concatenate(att, 0)).astype(BF16)
            upd = lax.dot_general(gated, wre[4], TN, preferred_element_type=F32)
            after.append(before[:, cc * 8 : cc * 8 + 8] + upd.reshape(nb, 8, 128))
        ns[blk, sub16] = jnp.concatenate(after, 1).astype(BF16)
        for cc in range(2):
            flat = after[cc].reshape(ib, 128).astype(BF16)
            logits = lax.dot_general(wdist_ref[...], flat, NT, preferred_element_type=F32) + db
            own_log[b, hf, cc * bins : (cc + 1) * bins, :] = logits.astype(BF16)

    def forward(t):
        part = rows.at[head, pl.ds(((y + 2 * ny - t - 1) % ny) * nb, nb)]
        wait_bytes(part, rsem.at[OUT + t])
        to_other(part, part, FWD + t).start()

    project()

    def step(t, carry):
        b = (y + t + 1) % ny

        wait_bytes(gath.at[1 - core, :, :, b], rsem.at[BIAS_C + t])
        repack(b)

        def two(hf, c2):
            @pl.when((hf == 1) & (t < ny - 2))
            def _():
                after_y(t + 2)

            @pl.when((hf == 1) & (t < ny - 1))
            def _():
                after_x(t + 1)

            attend(b, hf)

            part = pl.ds(pl.multiple_of(hf * 16, 16), 16)
            sem = OUT + t + jnp.where(t == ny - 1, hf, 0)

            def send_half(j, c3):
                target = b * nb + (me % nb + j) % nb
                to_row(ns.at[target, part], rows.at[head, me, part], sem, target).start()
                return c3

            lax.fori_loop(jnp.where(t == ny - 1, 1, 0), nb, send_half, 0)
            return c2

        lax.fori_loop(0, 2, two, 0)

        @pl.when(t == ny - 1)
        def _():
            for hf in range(2):
                part = pl.ds(hf * 16, 16)
                pltpu.make_async_copy(
                    ns.at[me, part], rows.at[head, me, part], rsem.at[OUT + ny - 1 + hf]
                ).start()

        to_other(own_log.at[b], logc.at[head, b], LOG).start()
        pltpu.make_async_copy(own_log.at[b], logc.at[head, b], rsem.at[X_IN]).start()

        @pl.when(t >= 1)
        def _():
            forward(t - 1)

        return carry

    lax.fori_loop(0, ny, step, 0)
    for hf in range(2):
        part = rows.at[head, pl.ds(y * nb, nb), pl.ds(hf * 16, 16)]
        wait_bytes(part, rsem.at[OUT + ny - 1 + hf])
        to_other(part, part, FWD + ny - 1).start()
    for t in range(ny):
        part = rows.at[other, pl.ds(((y + 2 * ny - t - 1) % ny) * nb, nb)]
        wait_bytes(part, rsem.at[FWD + t])
    wait_bytes(logc.at[other], rsem.at[LOG])
    wait_bytes(logc.at[head], rsem.at[X_IN])

    wait_bytes(xs.at[pl.ds(0, nb - 1)], ssem.at[PEERS_IN])
    for d in range(1, ny):
        wait_bytes(xs.at[pl.ds(0, nb)], ssem.at[PEERS_IN + d])
    for t in range(ny - 1):
        wait_bytes(ns.at[pl.ds(0, nb)], ssem.at[OUT + t])
    for hf in range(2):
        wait_bytes(ns.at[pl.ds(0, nb - 1), pl.ds(0, 16)], ssem.at[OUT + ny - 1 + hf])
    for t in range(ny):
        wait_bytes(ns.at[pl.ds(0, nb)], ssem.at[FWD + t])
    wait_bytes(own_log, ssem.at[LOG])
    wait_bytes(gath.at[0, 0, 0, :, pl.ds(0, nz - 1)], ssem.at[BIAS_Z])
    for t in range(ny):
        for d in range(1, ny):
            wait_bytes(gath.at[core, head, y, 0], ssem.at[BIAS_Y + t * (ny - 1) + d - 1])
        wait_bytes(gath.at[core, head, :, 0], ssem.at[BIAS_X + t])
        wait_bytes(gath.at[core, :, :, 0], ssem.at[BIAS_C + t])


def finish(nb, rows_ref, logc_ref, wdist_ref, dbias_ref, new_ref, dist_ref, turn):
    bins = wdist_ref.shape[0]
    bi = lax.broadcasted_iota(jnp.int32, (bins, bins), 0)
    bj = lax.broadcasted_iota(jnp.int32, (bins, bins), 1)
    db = jnp.sum(jnp.where(bi == bj, dbias_ref[...], 0.0), -1, keepdims=True)
    for a in range(2):
        for r in range(nb):
            turn[r * 64 + a * 32 : r * 64 + a * 32 + 32, :] = rows_ref[a, r].astype(F32)
    news = [turn[pl.ds(kk, nb * 8, stride=8), :].astype(BF16) for kk in range(8)]
    flat = jnp.concatenate(news, 0)
    own = (lax.dot_general(wdist_ref[...], flat, NT, preferred_element_type=F32) + db).astype(BF16)
    own = own.astype(F32)
    for kk in range(8):
        new_ref[kk] = news[kk]
        c = kk % 2
        mirrored = logc_ref[kk // 4, 0, (kk // 2) % 2, c * bins : (c + 1) * bins, :]
        mine = own[:, kk * nb * 8 : (kk + 1) * nb * 8]
        dist_ref[kk] = (mine + mirrored.astype(F32)).astype(BF16)


def shards(
    pair_act,
    chain_id,
    residue_mask,
    norm_gain,
    w_proj,
    w_bias,
    chain_bias,
    w_out,
    w_dist,
    dist_bias,
):
    _, n, width = pair_act.shape
    nr = n // 8
    ny, nz = SHAPE[nr]
    bins = w_dist.shape[1]
    ib = n // ny
    nb = nr // ny
    vmem = pl.BlockSpec(memory_space=pltpu.VMEM)
    smem = pl.BlockSpec(memory_space=pltpu.SMEM)
    hbm = pl.BlockSpec(memory_space=pl.ANY)
    wdist_t = w_dist.T
    dbias = dist_bias.reshape(1, bins)
    rows, logc = pl.pallas_call(
        functools.partial(kernel, ny, nz),
        out_shape=(
            jax.ShapeDtypeStruct((2, nr, 32, width), BF16),
            jax.ShapeDtypeStruct((2, ny, 2, 2 * bins, ib), BF16),
        ),
        in_specs=[hbm, vmem, vmem, vmem, vmem, vmem, smem, vmem, vmem, vmem],
        out_specs=(hbm, hbm),
        scratch_shapes=[
            pltpu.VMEM((8, n, width), BF16),
            pltpu.VMEM((n * 8, width), F32),
            pltpu.VMEM((nr, 32, width), BF16),
            pltpu.VMEM((nr, 32, width), BF16),
            pltpu.VMEM((2, 2, ny, ny, nz, 16, ib), BF16),
            pltpu.VMEM((2, n, 2 * ib), F32),
            pltpu.VMEM((2, 8, n), F32),
            pltpu.VMEM((2 * width, 128), BF16),
            pltpu.VMEM((64, width), BF16),
            pltpu.VMEM((5, width, width), BF16),
            pltpu.VMEM((4, ny, width, ib), BF16),
            pltpu.VMEM((4, n, width), BF16),
            pltpu.VMEM((4, 2, 80, n), BF16),
            pltpu.VMEM((4, ny, width, ib), F32),
            pltpu.VMEM((nr, 32, width), BF16),
            pltpu.VMEM((ny, 2, 2 * bins, ib), BF16),
            pltpu.SemaphoreType.DMA((N_SEM,)),
            pltpu.SemaphoreType.DMA((N_SEM,)),
            pltpu.SemaphoreType.REGULAR,
        ],
        compiler_params=pltpu.CompilerParams(
            collective_id=0, has_side_effects=True, vmem_limit_bytes=60 << 20
        ),
        name="triangle",
    )(
        pair_act,
        chain_id.reshape(1, n),
        residue_mask.reshape(1, n),
        norm_gain.reshape(1, width),
        w_proj.reshape(2 * width, 128),
        w_bias.T,
        chain_bias,
        w_out.reshape(64, width),
        wdist_t,
        dbias,
    )
    new, dist = pl.pallas_call(
        functools.partial(finish, nb),
        grid=(ny,),
        out_shape=(
            jax.ShapeDtypeStruct((8, n, width), BF16),
            jax.ShapeDtypeStruct((8, bins, n), BF16),
        ),
        in_specs=[
            pl.BlockSpec((2, nb, 32, width), lambda q: (0, q, 0, 0)),
            pl.BlockSpec((2, 1, 2, 2 * bins, ib), lambda q: (0, q, 0, 0, 0)),
            pl.BlockSpec((bins, width), lambda q: (0, 0)),
            pl.BlockSpec((1, bins), lambda q: (0, 0)),
        ],
        out_specs=(
            pl.BlockSpec((8, ib, width), lambda q: (0, q, 0)),
            pl.BlockSpec((8, bins, ib), lambda q: (0, 0, q)),
        ),
        scratch_shapes=[pltpu.VMEM((nb * 64, width), F32)],
        compiler_params=pltpu.CompilerParams(vmem_limit_bytes=62 << 20),
        name="finish",
    )(rows, logc, wdist_t, dbias)
    return new, jnp.transpose(dist, (0, 2, 1))


def solution(mesh):
    in_specs = (
        P(("dp", "row"), None, None),
        P("dp"),
        P("dp"),
        P(),
        P(None, "head", None),
        P(None, "head"),
        P(None, "head"),
        P("head", None, None),
        P(),
        P(),
    )
    out_specs = (P(("dp", "row"), None, None), P(("dp", "row"), None, None))
    return jax.shard_map(shards, mesh=mesh, in_specs=in_specs, out_specs=out_specs, check_vma=False)
```
